32 devices in a mesh: groups: 2 (over x), ta: 16 (over z, y, core).
Axes of the slice: x: 2, y: 2, z: 4, core: 2. Of those that a mesh axis runs over, the one named last changes fastest.
Arguments:
- gauge_links: float32 [4, 4, 256, 512], P(None, None, ('groups', 'ta')), parts along dimension 2, may hold values from -1 to 1, as said below
- cotangent: float32 [4, 4, 256, 512], P(None, None, ('groups', 'ta')), parts along dimension 2, may hold values from -6 to 6
- conv_weight: float32 [16, 243], replicated, may hold values from -0.375 to 0.375
- conv_bias: float32 [16], replicated, may hold values from -3 to 3
- head_weight: float32 [10, 16], replicated, may hold values from -1.5 to 1.5
- head_bias: float32 [10], replicated, may hold values from -3 to 3
- site_mask: int32 [256, 512], P(('groups', 'ta')), parts along dimension 0, may hold values from 0 to 1, as said below
- direction: int32 [4], replicated, may hold values from 0 to 3, each once
Outputs:
- grad_links: float32 [4, 4, 256, 512], P(None, None, ('groups', 'ta')), parts along dimension 2
- grad_conv_weight: float32 [32, 243], P('groups'), parts along dimension 0
- grad_conv_bias: float32 [32], P('groups'), parts along dimension 0
- grad_head_weight: float32 [20, 16], P('groups'), parts along dimension 0
- grad_head_bias: float32 [20], P('groups'), parts along dimension 0
The draws below stay inside these ranges and needn't reach their ends.
There are 2 independent parts, one for each index of `groups`. The reference program is written for one: setup_inputs(seed, part) draws one part's arguments, and reference() takes and returns one part's arrays. A program takes and returns all parts, laid end to end along the dimension named above; an argument that names none is the same for every part. Nothing has to cross between parts.
Inputs may be any that keep to these rules, and one draw needn't show every extreme that they name: `gauge_links`: every link is a unit quaternion. `site_mask`: 1 only at sites whose coordinate sum t + x1 + x2 + x3 has one parity, the same over the whole lattice.
All inputs are finite; a program needn't handle non-finite values.
Results may differ from the reference program's by a relative error of at most 0.0003.
Values sent between devices are 32-bit elements; how exact they have to be, the bound alone decides.
A program may use at most 128 MiB of HBM per device.

```python
import math
from functools import partial
import jax
import jax.numpy as jnp
from jax import lax

HID = 16
FEAT = 3
TAPS = 81
LS = 8
COEF = 10
TIME = 128
SITES = 65536


def draw_gauge_links(key, part):
    subkeys = jax.random.split(key, 3)
    layout = (4, TIME, LS ** 3)
    mixing = jax.random.uniform(subkeys[0], layout, jnp.float32)
    polar_angle = jnp.arcsin(jnp.sqrt(mixing))
    first_angle = jax.random.uniform(subkeys[1], layout, jnp.float32, -math.pi, math.pi)
    second_angle = jax.random.uniform(subkeys[2], layout, jnp.float32, -math.pi, math.pi)
    return jnp.stack([jnp.cos(polar_angle) * jnp.cos(first_angle), jnp.cos(polar_angle) * jnp.sin(first_angle), jnp.sin(polar_angle) * jnp.cos(second_angle), jnp.sin(polar_angle) * jnp.sin(second_angle)], axis=1)


def draw_site_mask(key, part):
    parity_bit = jax.random.randint(jax.random.fold_in(key, 11), (), 0, 2)
    keep = jax.random.randint(jax.random.fold_in(key, 12), (TIME, LS ** 3), 0, 4) > 0
    time_index = lax.iota(jnp.int32, TIME)
    site_index = lax.iota(jnp.int32, LS ** 3)
    coord_sum = time_index[:, None] + site_index[None, :] // (LS * LS) + site_index[None, :] // LS % LS + site_index[None, :] % LS
    chosen = (coord_sum % 2 == parity_bit) & keep
    return chosen.astype(jnp.int32)


def steps_of(stream_key, shape, cuts, low, top_value):
    loudness, own = 1.0, jax.random.fold_in(stream_key, 6)
    for dim, parts in cuts:
        steps = jnp.exp(jax.random.uniform(jax.random.fold_in(own, dim), (parts,), jnp.float32, low / len(cuts), top_value / len(cuts)))
        loudness = loudness * jnp.repeat(steps, shape[dim] // parts).reshape([-1 if axis == dim else 1 for axis in range(len(shape))])
    return loudness


def gaussian(stream_key, dims, width, reach, shards=(), held_as=jnp.bfloat16):
    result = jax.random.normal(stream_key, dims, jnp.float32) * width
    if len(shards) > 0:
        result = steps_of(stream_key, dims, shards, -0.22, 0.18) * result
    return jnp.clip(result, min=-reach, max=reach).astype(held_as)


def setup_inputs(seed: int = 0, part: int = 0) -> dict:
    keys = jax.random.split(jax.random.key(seed), 9)
    own_keys = jax.random.split(jax.random.fold_in(keys[8], part), 9)
    return {
        "gauge_links": draw_gauge_links(jax.random.fold_in(jax.random.fold_in(keys[8], part), 71), part),
        "cotangent": gaussian(own_keys[1], (4, 4, TIME, LS**3), 1.0, 6.0, ((2, 16),), jnp.float32),
        "conv_weight": gaussian(keys[2], (HID, TAPS * FEAT), (TAPS * FEAT) ** -0.5, 0.375, (), jnp.float32),
        "conv_bias": gaussian(keys[3], (HID,), 0.5, 3.0, (), jnp.float32),
        "head_weight": gaussian(keys[4], (COEF, HID), HID ** -0.5, 1.5, (), jnp.float32),
        "head_bias": gaussian(keys[5], (COEF,), 0.5, 3.0, (), jnp.float32),
        "site_mask": draw_site_mask(jax.random.fold_in(jax.random.fold_in(keys[8], part), 71), part),
        "direction": jax.random.permutation(keys[7], 4).astype(jnp.int32),
    }


HIGH = lax.Precision.HIGHEST

def quat_mul(former, latter):
    return jnp.stack([former[0] * latter[0] - former[1] * latter[1] - former[2] * latter[2] - former[3] * latter[3], former[0] * latter[1] + former[1] * latter[0] + former[2] * latter[3] - former[3] * latter[2], former[0] * latter[2] - former[1] * latter[3] + former[2] * latter[0] + former[3] * latter[1], former[0] * latter[3] + former[1] * latter[2] - former[2] * latter[1] + former[3] * latter[0]])

def quat_conj(factor):
    return jnp.stack([factor[0], -factor[1], -factor[2], -factor[3]])

def step_time(values, offset):
    return jnp.roll(values, -offset, axis=-2)

def step_first(values, offset, extent):
    return jnp.roll(values, -offset * extent * extent, axis=-1)

def step_second(values, offset, extent):
    layout = values.shape
    folded = values.reshape(layout[:-1] + (extent, extent * extent))
    return jnp.roll(folded, -offset * extent, axis=-1).reshape(layout)

def step_third(values, offset, extent):
    column = lax.iota(jnp.int32, extent ** 3) % extent
    if offset > 0:
        return jnp.where(column == extent - 1, jnp.roll(values, extent - 1, axis=-1), jnp.roll(values, -1, axis=-1))
    return jnp.where(column == 0, jnp.roll(values, 1 - extent, axis=-1), jnp.roll(values, 1, axis=-1))

def displace(values, axis_index, offset, extent):
    branches = [partial(step_time, offset=offset), partial(step_first, offset=offset, extent=extent), partial(step_second, offset=offset, extent=extent), partial(step_third, offset=offset, extent=extent)]
    if isinstance(axis_index, int):
        return branches[axis_index](values)
    return lax.switch(axis_index, branches, values)

def pick(values, index):
    return lax.dynamic_index_in_dim(values, index, 0, keepdims=False)

def staple_sum(link_field, order, extent):
    active = order[0]
    active_link = pick(link_field, active)
    summed = jnp.zeros_like(active_link)
    for partner in (1, 2, 3):
        across = order[partner]
        across_link = pick(link_field, across)
        upper_loop = quat_mul(quat_mul(displace(across_link, active, 1, extent), quat_conj(displace(active_link, across, 1, extent))), quat_conj(across_link))
        nu_back = displace(across_link, across, -1, extent)
        lower_loop = quat_mul(quat_mul(quat_conj(displace(nu_back, active, 1, extent)), quat_conj(displace(active_link, across, -1, extent))), nu_back)
        summed = summed + upper_loop + lower_loop
    return summed

def plaquette_traces(link_field, order, extent):
    other_dirs = [order[partner] for partner in (1, 2, 3)]
    others = [pick(link_field, other) for other in other_dirs]
    traces = []
    for former_idx, latter_idx in ((0, 1), (0, 2), (1, 2)):
        left_path = quat_mul(others[former_idx], displace(others[latter_idx], other_dirs[former_idx], 1, extent))
        right_path = quat_mul(others[latter_idx], displace(others[former_idx], other_dirs[latter_idx], 1, extent))
        traces.append(lax.optimization_barrier(jnp.sum(left_path * right_path, axis=0)))
    return jnp.stack(traces)

def cardinal(spot):
    rising = 0.5 * spot * spot
    middle = 0.5 * (-2.0 * spot * spot + 6.0 * spot - 3.0)
    falling = 0.5 * (3.0 - spot) * (3.0 - spot)
    return jnp.where(spot < 0.0, 0.0, jnp.where(spot < 1.0, rising, jnp.where(spot < 2.0, middle, jnp.where(spot < 3.0, falling, 0.0))))

def spline_gain(cosine, coeffs):
    number = coeffs.shape[0]
    scaled = (cosine + 1.0) * (0.5 * (number - 2))
    knot_pos = jnp.arange(number, dtype=cosine.dtype).reshape(-1, 1, 1)
    spline_basis = cardinal(scaled[None] - knot_pos + 2.0)
    return jnp.tanh(lax.optimization_barrier(jnp.sum(coeffs * spline_basis, axis=0)))

def rotate(active_link, staple, coeffs):
    closed_loop = quat_mul(active_link, staple)
    cosine = closed_loop[0] / 6.0
    generator = jnp.stack([jnp.zeros_like(closed_loop[0]), closed_loop[1], closed_loop[2], closed_loop[3]])
    turned = quat_mul(generator, active_link)
    strength = spline_gain(cosine, coeffs)
    length_sq = closed_loop[1] * closed_loop[1] + closed_loop[2] * closed_loop[2] + closed_loop[3] * closed_loop[3]
    return (active_link + strength * turned) * lax.rsqrt(1.0 + strength * strength * length_sq)

def tap_shift(values, offsets, extent):
    for axis_index, offset in enumerate(offsets):
        if offset != 0:
            values = displace(values, axis_index, offset, extent)
    return values

def conditioner(features, w_conv, b_conv, w_head, b_head, extent):
    channels = features.shape[0]
    preact = jnp.zeros((w_conv.shape[0], features.shape[1] * features.shape[2]), jnp.float32)
    tap_index = 0
    for time_off in (-1, 0, 1):
        for first_off in (-1, 0, 1):
            for second_off in (-1, 0, 1):
                for third_off in (-1, 0, 1):
                    shifted = tap_shift(features, (time_off, first_off, second_off, third_off), extent)
                    preact = preact + jnp.dot(w_conv[:, channels * tap_index:channels * tap_index + channels], shifted.reshape(channels, -1), precision=HIGH, preferred_element_type=jnp.float32)
                    tap_index += 1
    hidden = jnp.tanh(preact + b_conv[:, None])
    head_out = jnp.dot(w_head, hidden, precision=HIGH, preferred_element_type=jnp.float32) + b_head[:, None]
    return head_out.reshape((w_head.shape[0], features.shape[1], features.shape[2]))

def reference(gauge_links, cotangent, conv_weight, conv_bias, head_weight, head_bias, site_mask, direction):
    active = direction[0]
    active_mask = site_mask != 0

    def forward(link_field, w_conv, b_conv, w_head, b_head):
        features = plaquette_traces(link_field, direction, LS)
        coeffs = conditioner(features, w_conv, b_conv, w_head, b_head, LS)
        active_link = pick(link_field, active)
        rotated = rotate(active_link, staple_sum(link_field, direction, LS), coeffs)
        updated = jnp.where(active_mask[None], rotated, active_link)
        return lax.dynamic_update_index_in_dim(link_field, updated, active, 0)
    _, pullback = jax.vjp(forward, gauge_links, conv_weight, conv_bias, head_weight, head_bias)
    gradients = pullback(cotangent)
    normalizer = 1.0 / math.sqrt(SITES)
    return (gradients[0], gradients[1] * normalizer, gradients[2] * normalizer, gradients[3] * normalizer, gradients[4] * normalizer)
```

```python
from functools import partial
import math

import jax
import jax.numpy as jnp
import numpy as np
from jax import lax
from jax.experimental import pallas as pl
from jax.experimental.pallas import tpu as pltpu
from jax.sharding import PartitionSpec as P

LS = 8
SITES = LS**3
OWN = 8
REACH = 3
ROWS = 16
HID = 16
FEAT = 3
COEF = 10
SPACE_TAPS = 27
GROUP = FEAT * ROWS
BANK = 1408
HIGH = lax.Precision.HIGHEST
NT = (((1,), (1,)), ((), ()))
TN = (((0,), (0,)), ((), ()))
NN = (((1,), (0,)), ((), ()))


def lane_roll(values, by):
    by = by % 128
    return jnp.concatenate(
        [pltpu.roll(values[:, at : at + 128], by, 1) for at in range(0, values.shape[1], 128)],
        axis=1,
    )


def moved(values, axis, offset):
    if axis == 0:
        return pltpu.roll(values, -offset % values.shape[0], 0)
    if axis == 1:
        return pltpu.roll(values, -offset * LS * LS % SITES, 1)
    stride = LS if axis == 2 else 1
    lane = lax.broadcasted_iota(jnp.int32, values.shape, 1)
    coordinate = (lane // stride) % LS
    wraps = coordinate == (LS - 1 if offset > 0 else 0)
    return jnp.where(
        wraps,
        lane_roll(values, offset * (LS - 1) * stride),
        lane_roll(values, -offset * stride),
    )


@partial(jax.custom_vjp, nondiff_argnums=(1, 2))
def shift(values, axis, offset):
    return moved(values, axis, offset)


shift.defvjp(
    lambda values, axis, offset: (moved(values, axis, offset), None),
    lambda axis, offset, _, grad: (moved(grad, axis, -offset),),
)


def q_shift(q, axis, offset):
    return tuple(shift(part, axis, offset) for part in q)


def q_mul(p, q):
    return (
        p[0] * q[0] - p[1] * q[1] - p[2] * q[2] - p[3] * q[3],
        p[0] * q[1] + p[1] * q[0] + p[2] * q[3] - p[3] * q[2],
        p[0] * q[2] - p[1] * q[3] + p[2] * q[0] + p[3] * q[1],
        p[0] * q[3] + p[1] * q[2] - p[2] * q[1] + p[3] * q[0],
    )


def q_conj(q):
    return (q[0], -q[1], -q[2], -q[3])


def staples(links, m):
    total = None
    for n in range(4):
        if n == m:
            continue
        ahead = q_shift(links[n], m, 1)
        upper = q_mul(q_mul(ahead, q_conj(q_shift(links[m], n, 1))), q_conj(links[n]))
        lower = q_shift(q_mul(q_conj(q_mul(links[m], ahead)), links[n]), n, -1)
        both = tuple(a + b for a, b in zip(upper, lower))
        total = both if total is None else tuple(a + b for a, b in zip(total, both))
    return total


def traces(links, m):
    others = [n for n in range(4) if n != m]
    out = []
    for i, j in ((0, 1), (0, 2), (1, 2)):
        a, b = others[i], others[j]
        left = q_mul(links[a], q_shift(links[b], a, 1))
        right = q_mul(links[b], q_shift(links[a], b, 1))
        out.append(sum(x * y for x, y in zip(left, right)))
    return tuple(out)


def cardinal(spot):
    rising = 0.5 * spot * spot
    middle = 0.5 * (-2.0 * spot * spot + 6.0 * spot - 3.0)
    falling = 0.5 * (3.0 - spot) * (3.0 - spot)
    return jnp.where(
        spot < 0.0,
        0.0,
        jnp.where(
            spot < 1.0, rising, jnp.where(spot < 2.0, middle, jnp.where(spot < 3.0, falling, 0.0))
        ),
    )


def rotate(link, staple, coeffs):
    loop = q_mul(link, staple)
    scaled = (loop[0] / 6.0 + 1.0) * (0.5 * (COEF - 2))
    strength = jnp.tanh(sum(coeffs[j] * cardinal(scaled - j + 2.0) for j in range(COEF)))
    turned = q_mul((jnp.zeros_like(loop[0]), loop[1], loop[2], loop[3]), link)
    length_sq = loop[1] * loop[1] + loop[2] * loop[2] + loop[3] * loop[3]
    scale = lax.rsqrt(1.0 + strength * strength * length_sq)
    return tuple((u + strength * v) * scale for u, v in zip(link, turned))


def halves(values):
    high = values.astype(jnp.bfloat16)
    return high, (values - high.astype(jnp.float32)).astype(jnp.bfloat16)


def dot3(a, b, dims):
    def one(x, y):
        return lax.dot_general(x, y, dims, preferred_element_type=jnp.float32)

    return one(a[0], b[0]) + (one(a[0], b[1]) + one(a[1], b[0]))


def group_roll(values, by):
    by = by % ROWS
    if by == 0:
        return values
    lane = lax.broadcasted_iota(jnp.int32, values.shape, 1) % ROWS
    return jnp.where(lane >= by, lane_roll(values, by), lane_roll(values, by - ROWS))


def kernel(
    m_ref, links_ref, halo_ref, cot_ref, mask_ref, w0_ref, head_ref, cb_ref, hb_ref,
    grad_ref, dw_ref, dcb_ref, dhw_ref, dhb_ref,
    feat_ref, staple_ref, link_ref, bank_hi, bank_lo, big_hi, big_lo, dbank_ref,
):
    m = m_ref[0]

    def load(d):
        return tuple(
            jnp.concatenate([links_ref[d, c], halo_ref[4 * d + c]], axis=0) for c in range(4)
        )

    for case in range(4):

        @pl.when(m == case)
        def _(case=case):
            links = tuple(load(d) for d in range(4))
            for k, value in enumerate(traces(links, case)):
                feat_ref[k * ROWS : (k + 1) * ROWS, :] = value
            for c, value in enumerate(staples(links, case)):
                staple_ref[c] = value

    w0 = w0_ref[...]
    for r in range(ROWS):
        high, low = halves(group_roll(w0, r))
        big_hi[r * HID : (r + 1) * HID, :] = high
        big_lo[r * HID : (r + 1) * HID, :] = low

    used = SPACE_TAPS * GROUP
    bank_hi[used:, :] = jnp.zeros((BANK - used, SITES), jnp.bfloat16)
    bank_lo[used:, :] = jnp.zeros((BANK - used, SITES), jnp.bfloat16)
    features = feat_ref[...]
    for c in (-1, 0, 1):
        third = moved(features, 3, c) if c else features
        for b in (-1, 0, 1):
            second = moved(third, 2, b) if b else third
            for a in (-1, 0, 1):
                first = moved(second, 1, a) if a else second
                e = ((a + 1) * 3 + b + 1) * 3 + c + 1
                high, low = halves(first)
                bank_hi[e * GROUP : (e + 1) * GROUP, :] = high
                bank_lo[e * GROUP : (e + 1) * GROUP, :] = low

    bank = (bank_hi[...], bank_lo[...])
    big = (big_hi[...], big_lo[...])
    hidden = jnp.tanh(dot3(big, bank, NN) + cb_ref[...])
    hidden2 = halves(hidden)
    head2 = halves(head_ref[...])
    coeffs = dot3(head2, hidden2, NN) + hb_ref[...]

    row = lax.broadcasted_iota(jnp.int32, (ROWS, SITES), 0)
    mask = jnp.concatenate([mask_ref[...], halo_ref[20]], axis=0)
    inside = (row <= OWN) | (row >= ROWS - 2)
    chosen = (mask != 0.0) & inside
    active = tuple(
        jnp.concatenate([links_ref[m, c], halo_ref[4 * m + c]], axis=0) for c in range(4)
    )
    cot = tuple(jnp.concatenate([cot_ref[m, c], halo_ref[16 + c]], axis=0) for c in range(4))
    _, pull = jax.vjp(
        rotate,
        active,
        tuple(staple_ref[c] for c in range(4)),
        tuple(coeffs[j * ROWS : (j + 1) * ROWS, :] for j in range(COEF)),
    )
    dlink, dstaple, dcoeff = pull(tuple(jnp.where(chosen, g, 0.0) for g in cot))
    for c in range(4):
        link_ref[c] = jnp.where(chosen, dlink[c], cot[c])[:OWN, :]
        staple_ref[c] = dstaple[c]
    dcoeff = jnp.concatenate(dcoeff, axis=0)
    dcoeff2 = halves(dcoeff)
    wide = lax.broadcasted_iota(jnp.int32, (COEF * ROWS, ROWS * HID), 1)
    tall = lax.broadcasted_iota(jnp.int32, (COEF * ROWS, ROWS * HID), 0)
    keep = (tall % ROWS == wide // HID) & (wide < OWN * HID)
    dhead = jnp.where(keep, dot3(dcoeff2, hidden2, NT), 0.0)
    fold = (
        lax.broadcasted_iota(jnp.int32, (ROWS * HID, 128), 0) % HID
        == lax.broadcasted_iota(jnp.int32, (ROWS * HID, 128), 1)
    ).astype(jnp.float32)
    folded = lax.dot_general(dhead, fold, NN, precision=HIGH, preferred_element_type=jnp.float32)
    dhw_ref[...] = jnp.concatenate(
        [jnp.sum(folded[j * ROWS : j * ROWS + OWN], axis=0, keepdims=True) for j in range(COEF)],
        axis=0,
    )
    own_sum = jnp.concatenate(
        [
            jnp.sum(dcoeff[j * ROWS : j * ROWS + OWN], axis=0, keepdims=True)
            for j in range(COEF)
        ],
        axis=0,
    )
    dhb_ref[...] = jnp.sum(own_sum, axis=1, keepdims=True)

    dpre = dot3(head2, dcoeff2, TN) * (1.0 - hidden * hidden)
    own_pre = dpre[: OWN * HID]
    pre_sum = sum(own_pre[r * HID : (r + 1) * HID] for r in range(OWN))
    dcb_ref[...] = jnp.sum(pre_sum, axis=1, keepdims=True)
    dpre2 = halves(dpre)
    dbig = dot3((dpre2[0][: OWN * HID], dpre2[1][: OWN * HID]), bank, NT)
    dw_ref[...] = sum(group_roll(dbig[r * HID : (r + 1) * HID], -r) for r in range(OWN))

    dbank_ref[...] = dot3(big, dpre2, TN)
    dfeat = None
    for c in (-1, 0, 1):
        third = None
        for b in (-1, 0, 1):
            second = None
            for a in (-1, 0, 1):
                e = ((a + 1) * 3 + b + 1) * 3 + c + 1
                part = dbank_ref[e * GROUP : (e + 1) * GROUP, :]
                part = moved(part, 1, -a) if a else part
                second = part if second is None else second + part
            second = moved(second, 2, -b) if b else second
            third = second if third is None else third + second
        third = moved(third, 3, -c) if c else third
        dfeat = third if dfeat is None else dfeat + third
    feat_ref[...] = dfeat

    for case in range(4):

        @pl.when(m == case)
        def _(case=case):
            links = tuple(load(d) for d in range(4))
            _, back = jax.vjp(lambda u: (traces(u, case), staples(u, case)), links)
            (dlinks,) = back(
                (
                    tuple(feat_ref[k * ROWS : (k + 1) * ROWS, :] for k in range(FEAT)),
                    tuple(staple_ref[c] for c in range(4)),
                )
            )
            for d in range(4):
                for c in range(4):
                    base = link_ref[c] if d == case else cot_ref[d, c]
                    grad_ref[d, c] = base + dlinks[d][c][:OWN, :]


def spread():
    table = np.zeros((3 * SPACE_TAPS * FEAT, BANK), np.float32)
    for a in range(3):
        for e in range(SPACE_TAPS):
            for k in range(FEAT):
                table[(a * SPACE_TAPS + e) * FEAT + k, e * GROUP + k * ROWS + (a - 1) % ROWS] = 1.0
    return table


def body(
    gauge_links, cotangent, conv_weight, conv_bias, head_weight, head_bias, site_mask, direction
):
    active = direction[0]
    mask = (site_mask != 0).astype(jnp.float32)
    active_cot = lax.dynamic_index_in_dim(cotangent, active, 0, keepdims=False)

    def message(rows):
        return jnp.concatenate(
            [
                gauge_links[:, :, rows].reshape(16, REACH, SITES),
                active_cot[:, rows],
                mask[None, rows],
            ],
            axis=0,
        )

    count = lax.axis_size("ta")
    ahead = lax.ppermute(
        message(slice(0, REACH)), "ta", [((i + 1) % count, i) for i in range(count)]
    )
    behind = lax.ppermute(
        message(slice(OWN - REACH, OWN)), "ta", [(i, (i + 1) % count) for i in range(count)]
    )
    halo = jnp.concatenate(
        [ahead, jnp.zeros((21, ROWS - OWN - 2 * REACH, SITES), jnp.float32), behind], axis=1
    )

    dropped = direction[jnp.array([3, 2, 1])]
    below = jnp.sum(
        (direction[1:][None, :] < dropped[:, None]).astype(jnp.int32), axis=1
    )
    perm = ((2 - below)[:, None] == jnp.arange(3)[None, :]).astype(jnp.float32)
    table = jnp.asarray(spread())
    sorted_weight = jnp.sum(
        conv_weight.reshape(HID, 3 * SPACE_TAPS, FEAT, 1) * perm[None, None], axis=2
    ).reshape(HID, 3 * SPACE_TAPS * FEAT)
    w0 = jnp.dot(sorted_weight, table, precision=HIGH)
    eye = jnp.eye(ROWS, dtype=jnp.float32)
    head = (head_weight[:, None, None, :] * eye[None, :, :, None]).reshape(
        COEF * ROWS, ROWS * HID
    )
    cb = jnp.tile(conv_bias, ROWS).reshape(ROWS * HID, 1)
    hb = jnp.repeat(head_bias, ROWS).reshape(COEF * ROWS, 1)

    vmem = pl.BlockSpec(memory_space=pltpu.VMEM)
    f32, bf16 = jnp.float32, jnp.bfloat16
    grad, dw0, dcb, dhw, dhb = pl.pallas_call(
        kernel,
        out_shape=(
            jax.ShapeDtypeStruct((4, 4, OWN, SITES), f32),
            jax.ShapeDtypeStruct((HID, BANK), f32),
            jax.ShapeDtypeStruct((HID, 1), f32),
            jax.ShapeDtypeStruct((COEF, 128), f32),
            jax.ShapeDtypeStruct((COEF, 1), f32),
        ),
        in_specs=[pl.BlockSpec(memory_space=pltpu.SMEM)] + [vmem] * 8,
        out_specs=(vmem,) * 5,
        scratch_shapes=[
            pltpu.VMEM((GROUP, SITES), f32),
            pltpu.VMEM((4, ROWS, SITES), f32),
            pltpu.VMEM((4, OWN, SITES), f32),
            pltpu.VMEM((BANK, SITES), bf16),
            pltpu.VMEM((BANK, SITES), bf16),
            pltpu.VMEM((ROWS * HID, BANK), bf16),
            pltpu.VMEM((ROWS * HID, BANK), bf16),
            pltpu.VMEM((BANK, SITES), f32),
        ],
        compiler_params=pltpu.CompilerParams(vmem_limit_bytes=40 * 2**20),
    )(direction, gauge_links, halo, cotangent, mask, w0, head, cb, hb)

    dweight = lax.dot_general(dw0, table, NT, precision=HIGH)
    summed = lax.psum((dweight, dcb[:, 0], dhw[:, :HID], dhb[:, 0]), "ta")
    dweight = jnp.sum(
        summed[0].reshape(HID, 3 * SPACE_TAPS, 1, FEAT) * perm[None, None], axis=3
    ).reshape(HID, 3 * SPACE_TAPS * FEAT)
    normalizer = 1.0 / math.sqrt(count * OWN * SITES)
    return (
        grad,
        dweight * normalizer,
        summed[1] * normalizer,
        summed[2] * normalizer,
        summed[3] * normalizer,
    )


def solution(mesh):
    return jax.shard_map(
        body,
        mesh=mesh,
        in_specs=(
            P(None, None, ("groups", "ta"), None),
            P(None, None, ("groups", "ta"), None),
            P(),
            P(),
            P(),
            P(),
            P(("groups", "ta"), None),
            P(),
        ),
        out_specs=(
            P(None, None, ("groups", "ta"), None),
            P("groups", None),
            P("groups"),
            P("groups", None),
            P("groups"),
        ),
        check_vma=False,
    )
```

```python
from functools import partial
import math

import jax
import jax.numpy as jnp
import numpy as np
from jax import lax
from jax.experimental import pallas as pl
from jax.experimental.pallas import tpu as pltpu
from jax.sharding import PartitionSpec as P

LS = 8
SITES = LS**3
OWN = 8
REACH = 3
ROWS = 16
HID = 16
FEAT = 3
COEF = 10
SPACE_TAPS = 27
GROUP = FEAT * ROWS
BANK = 1408
AT_CB = 3 * SPACE_TAPS * FEAT
AT_HEAD = AT_CB + 1
AT_HB = AT_HEAD + COEF
PACK = 256
HIGH = lax.Precision.HIGHEST
NT = (((1,), (1,)), ((), ()))
TN = (((0,), (0,)), ((), ()))
NN = (((1,), (0,)), ((), ()))


def lane_roll(values, by):
    by = by % 128
    return jnp.concatenate(
        [pltpu.roll(values[:, at : at + 128], by, 1) for at in range(0, values.shape[1], 128)],
        axis=1,
    )


def moved(values, axis, offset):
    if axis == 0:
        return pltpu.roll(values, -offset % values.shape[0], 0)
    if axis == 1:
        return pltpu.roll(values, -offset * LS * LS % SITES, 1)
    stride = LS if axis == 2 else 1
    lane = lax.broadcasted_iota(jnp.int32, values.shape, 1)
    coordinate = (lane // stride) % LS
    wraps = coordinate == (LS - 1 if offset > 0 else 0)
    return jnp.where(
        wraps,
        lane_roll(values, offset * (LS - 1) * stride),
        lane_roll(values, -offset * stride),
    )


@partial(jax.custom_vjp, nondiff_argnums=(1, 2))
def shift(values, axis, offset):
    return moved(values, axis, offset)


shift.defvjp(
    lambda values, axis, offset: (moved(values, axis, offset), None),
    lambda axis, offset, _, grad: (moved(grad, axis, -offset),),
)


def q_shift(q, axis, offset):
    return tuple(shift(part, axis, offset) for part in q)


def q_mul(p, q):
    return (
        p[0] * q[0] - p[1] * q[1] - p[2] * q[2] - p[3] * q[3],
        p[0] * q[1] + p[1] * q[0] + p[2] * q[3] - p[3] * q[2],
        p[0] * q[2] - p[1] * q[3] + p[2] * q[0] + p[3] * q[1],
        p[0] * q[3] + p[1] * q[2] - p[2] * q[1] + p[3] * q[0],
    )


def q_conj(q):
    return (q[0], -q[1], -q[2], -q[3])


def staples(links, m):
    total = None
    for n in range(4):
        if n == m:
            continue
        ahead = q_shift(links[n], m, 1)
        upper = q_mul(q_mul(ahead, q_conj(q_shift(links[m], n, 1))), q_conj(links[n]))
        lower = q_shift(q_mul(q_conj(q_mul(links[m], ahead)), links[n]), n, -1)
        both = tuple(a + b for a, b in zip(upper, lower))
        total = both if total is None else tuple(a + b for a, b in zip(total, both))
    return total


def traces(links, m):
    others = [n for n in range(4) if n != m]
    out = []
    for i, j in ((0, 1), (0, 2), (1, 2)):
        a, b = others[i], others[j]
        left = q_mul(links[a], q_shift(links[b], a, 1))
        right = q_mul(links[b], q_shift(links[a], b, 1))
        out.append(sum(x * y for x, y in zip(left, right)))
    return tuple(out)


def cardinal(spot):
    rising = 0.5 * spot * spot
    middle = 0.5 * (-2.0 * spot * spot + 6.0 * spot - 3.0)
    falling = 0.5 * (3.0 - spot) * (3.0 - spot)
    return jnp.where(
        spot < 0.0,
        0.0,
        jnp.where(
            spot < 1.0, rising, jnp.where(spot < 2.0, middle, jnp.where(spot < 3.0, falling, 0.0))
        ),
    )


def rotate(link, staple, coeffs):
    loop = q_mul(link, staple)
    scaled = (loop[0] / 6.0 + 1.0) * (0.5 * (COEF - 2))
    strength = jnp.tanh(sum(coeffs[j] * cardinal(scaled - j + 2.0) for j in range(COEF)))
    turned = q_mul((jnp.zeros_like(loop[0]), loop[1], loop[2], loop[3]), link)
    length_sq = loop[1] * loop[1] + loop[2] * loop[2] + loop[3] * loop[3]
    scale = lax.rsqrt(1.0 + strength * strength * length_sq)
    return tuple((u + strength * v) * scale for u, v in zip(link, turned))


def halves(values):
    high = values.astype(jnp.bfloat16)
    return high, (values - high.astype(jnp.float32)).astype(jnp.bfloat16)


def dot3(a, b, dims):
    def one(x, y):
        return lax.dot_general(x, y, dims, preferred_element_type=jnp.float32)

    return one(a[0], b[0]) + (one(a[0], b[1]) + one(a[1], b[0]))


def group_roll(values, by):
    by = by % ROWS
    if by == 0:
        return values
    lane = lax.broadcasted_iota(jnp.int32, values.shape, 1) % ROWS
    return jnp.where(lane >= by, lane_roll(values, by), lane_roll(values, by - ROWS))


def kernel(
    scale, m_ref, links_ref, halo_ref, cot_ref, mask_ref, cw_ref, table_ref, head_ref, cb_ref,
    hb_ref, grad_ref, pack_ref,
    feat_ref, staple_ref, link_ref, bank_hi, bank_lo, big_hi, big_lo, dbank_ref,
):
    m = m_ref[0]

    def load(d):
        return tuple(
            jnp.concatenate([links_ref[d, c], halo_ref[4 * d + c]], axis=0) for c in range(4)
        )

    def slots(case):
        others = [n for n in range(4) if n != case]
        found = []
        for missing in reversed(others):
            k = jnp.where(m_ref[3] == missing, 0, jnp.where(m_ref[2] == missing, 1, 2))
            found.append(pl.ds(pl.multiple_of(k * ROWS, ROWS), ROWS))
        return found

    for case in range(4):

        @pl.when(m == case)
        def _(case=case):
            links = tuple(load(d) for d in range(4))
            for at, value in zip(slots(case), traces(links, case)):
                feat_ref[at, :] = value
            for c, value in enumerate(staples(links, case)):
                staple_ref[c] = value

    w0 = lax.dot_general(
        cw_ref[...], table_ref[...], NN, precision=HIGH, preferred_element_type=jnp.float32
    )
    for r in range(ROWS):
        high, low = halves(group_roll(w0, r))
        big_hi[r * HID : (r + 1) * HID, :] = high
        big_lo[r * HID : (r + 1) * HID, :] = low

    used = SPACE_TAPS * GROUP
    bank_hi[used:, :] = jnp.zeros((BANK - used, SITES), jnp.bfloat16)
    bank_lo[used:, :] = jnp.zeros((BANK - used, SITES), jnp.bfloat16)
    features = feat_ref[...]
    for c in (-1, 0, 1):
        third = moved(features, 3, c) if c else features
        for b in (-1, 0, 1):
            second = moved(third, 2, b) if b else third
            for a in (-1, 0, 1):
                first = moved(second, 1, a) if a else second
                e = ((a + 1) * 3 + b + 1) * 3 + c + 1
                high, low = halves(first)
                bank_hi[e * GROUP : (e + 1) * GROUP, :] = high
                bank_lo[e * GROUP : (e + 1) * GROUP, :] = low

    bank = (bank_hi[...], bank_lo[...])
    big = (big_hi[...], big_lo[...])
    hidden = jnp.tanh(dot3(big, bank, NN) + cb_ref[...])
    hidden2 = halves(hidden)
    head2 = halves(head_ref[...])
    coeffs = dot3(head2, hidden2, NN) + hb_ref[...]

    row = lax.broadcasted_iota(jnp.int32, (ROWS, SITES), 0)
    mask = jnp.concatenate([mask_ref[...], halo_ref[20]], axis=0)
    inside = (row <= OWN) | (row >= ROWS - 2)
    chosen = (mask != 0.0) & inside
    active = tuple(
        jnp.concatenate([links_ref[m, c], halo_ref[4 * m + c]], axis=0) for c in range(4)
    )
    cot = tuple(jnp.concatenate([cot_ref[m, c], halo_ref[16 + c]], axis=0) for c in range(4))
    _, pull = jax.vjp(
        rotate,
        active,
        tuple(staple_ref[c] for c in range(4)),
        tuple(coeffs[j * ROWS : (j + 1) * ROWS, :] for j in range(COEF)),
    )
    dlink, dstaple, dcoeff = pull(tuple(jnp.where(chosen, g, 0.0) for g in cot))
    for c in range(4):
        link_ref[c] = jnp.where(chosen, dlink[c], cot[c])[:OWN, :]
        staple_ref[c] = dstaple[c]
    dcoeff = jnp.concatenate(dcoeff, axis=0)
    dcoeff2 = halves(dcoeff)
    wide = lax.broadcasted_iota(jnp.int32, (ROWS * HID, COEF * ROWS), 1)
    tall = lax.broadcasted_iota(jnp.int32, (ROWS * HID, COEF * ROWS), 0)
    keep = (wide % ROWS == tall // HID) & (tall < OWN * HID)
    dhead = jnp.where(keep, dot3(hidden2, dcoeff2, NT), 0.0)
    dhead = sum(dhead[r * HID : (r + 1) * HID] for r in range(OWN))
    fold = (
        lax.broadcasted_iota(jnp.int32, (COEF * ROWS, 128), 0) // ROWS + (AT_HEAD - 128)
        == lax.broadcasted_iota(jnp.int32, (COEF * ROWS, 128), 1)
    ).astype(jnp.float32)
    extra = lax.dot_general(dhead, fold, NN, precision=HIGH, preferred_element_type=jnp.float32)
    own_sum = jnp.concatenate(
        [
            jnp.sum(dcoeff[j * ROWS : j * ROWS + OWN], axis=0, keepdims=True)
            for j in range(COEF)
        ]
        + [jnp.zeros((HID - COEF, SITES), jnp.float32)],
        axis=0,
    )
    column = lax.broadcasted_iota(jnp.int32, (HID, 128), 1)
    extra += jnp.where(column == AT_HB - 128, jnp.sum(own_sum, axis=1, keepdims=True), 0.0)

    dpre = dot3(head2, dcoeff2, TN) * (1.0 - hidden * hidden)
    own_pre = dpre[: OWN * HID]
    pre_sum = sum(own_pre[r * HID : (r + 1) * HID] for r in range(OWN))
    extra += jnp.where(column == AT_CB - 128, jnp.sum(pre_sum, axis=1, keepdims=True), 0.0)
    dpre2 = halves(dpre)
    dbig = dot3((dpre2[0][: OWN * HID], dpre2[1][: OWN * HID]), bank, NT)
    dw0 = sum(group_roll(dbig[r * HID : (r + 1) * HID], -r) for r in range(OWN))
    dw = lax.dot_general(
        dw0, table_ref[...], NT, precision=HIGH, preferred_element_type=jnp.float32
    )
    pack_ref[:, :128] = dw[:, :128] * scale
    pack_ref[:, 128:] = (dw[:, 128:] + extra) * scale

    dbank_ref[...] = dot3(big, dpre2, TN)
    dfeat = None
    for c in (-1, 0, 1):
        third = None
        for b in (-1, 0, 1):
            second = None
            for a in (-1, 0, 1):
                e = ((a + 1) * 3 + b + 1) * 3 + c + 1
                part = dbank_ref[e * GROUP : (e + 1) * GROUP, :]
                part = moved(part, 1, -a) if a else part
                second = part if second is None else second + part
            second = moved(second, 2, -b) if b else second
            third = second if third is None else third + second
        third = moved(third, 3, -c) if c else third
        dfeat = third if dfeat is None else dfeat + third
    feat_ref[...] = dfeat

    for case in range(4):

        @pl.when(m == case)
        def _(case=case):
            links = tuple(load(d) for d in range(4))
            _, back = jax.vjp(lambda u: (traces(u, case), staples(u, case)), links)
            (dlinks,) = back(
                (
                    tuple(feat_ref[at, :] for at in slots(case)),
                    tuple(staple_ref[c] for c in range(4)),
                )
            )
            for d in range(4):
                for c in range(4):
                    base = link_ref[c] if d == case else cot_ref[d, c]
                    grad_ref[d, c] = base + dlinks[d][c][:OWN, :]


def spread():
    table = np.zeros((PACK, BANK), np.float32)
    for a in range(3):
        for e in range(SPACE_TAPS):
            for k in range(FEAT):
                table[(a * SPACE_TAPS + e) * FEAT + k, e * GROUP + k * ROWS + (a - 1) % ROWS] = 1.0
    return table


def sum_kernel(
    n, x_ref, out_ref, parts_ref, sums_ref, mine_ref, send1, recv1, send2, recv2
):
    me = lax.axis_index("ta")
    mesh_id = pl.DeviceIdType.MESH

    def to(k):
        return lax.rem(me + k, n)

    def scatter(k):
        return pltpu.make_async_remote_copy(
            src_ref=x_ref.at[to(k)],
            dst_ref=parts_ref.at[k],
            send_sem=send1.at[k],
            recv_sem=recv1.at[k],
            device_id={"ta": to(k)},
            device_id_type=mesh_id,
        )

    def gather(k):
        return pltpu.make_async_remote_copy(
            src_ref=mine_ref,
            dst_ref=sums_ref.at[k],
            send_sem=send2.at[k],
            recv_sem=recv2.at[k],
            device_id={"ta": to(k)},
            device_id_type=mesh_id,
        )

    def each(act):
        lax.fori_loop(1, n, lambda k, carry: (act(k), carry)[1], 0)

    barrier = pltpu.get_barrier_semaphore()
    each(
        lambda k: pl.semaphore_signal(
            barrier, inc=1, device_id={"ta": to(k)}, device_id_type=mesh_id
        )
    )
    pl.semaphore_wait(barrier, n - 1)
    each(lambda k: scatter(k).start())
    each(lambda k: scatter(k).wait_recv())
    total = x_ref[me]
    for k in range(1, n):
        total = total + parts_ref[k]
    mine_ref[...] = total
    each(lambda k: gather(k).start())
    out_ref[me] = total

    def keep(k):
        gather(k).wait_recv()
        out_ref[lax.rem(me + n - k, n)] = sums_ref[k]

    each(keep)
    each(lambda k: scatter(k).wait_send())
    each(lambda k: gather(k).wait_send())


def body(
    gauge_links, cotangent, conv_weight, conv_bias, head_weight, head_bias, site_mask, direction
):
    active = direction[0]
    mask = (site_mask != 0).astype(jnp.float32)
    active_cot = lax.dynamic_index_in_dim(cotangent, active, 0, keepdims=False)

    def message(rows):
        return jnp.concatenate(
            [
                gauge_links[:, :, rows].reshape(16, REACH, SITES),
                active_cot[:, rows],
                mask[None, rows],
            ],
            axis=0,
        )

    count = lax.axis_size("ta")
    ahead = lax.ppermute(
        message(slice(0, REACH)), "ta", [((i + 1) % count, i) for i in range(count)]
    )
    behind = lax.ppermute(
        message(slice(OWN - REACH, OWN)), "ta", [(i, (i + 1) % count) for i in range(count)]
    )
    halo = jnp.concatenate(
        [ahead, jnp.zeros((21, ROWS - OWN - 2 * REACH, SITES), jnp.float32), behind], axis=1
    )

    table = jnp.asarray(spread())
    weight = jnp.pad(conv_weight, ((0, 0), (0, PACK - AT_CB)))
    eye = jnp.eye(ROWS, dtype=jnp.float32)
    head = (head_weight[:, None, None, :] * eye[None, :, :, None]).reshape(
        COEF * ROWS, ROWS * HID
    )
    cb = jnp.tile(conv_bias, ROWS).reshape(ROWS * HID, 1)
    hb = jnp.repeat(head_bias, ROWS).reshape(COEF * ROWS, 1)

    vmem = pl.BlockSpec(memory_space=pltpu.VMEM)
    f32, bf16 = jnp.float32, jnp.bfloat16
    grad, packed = pl.pallas_call(
        partial(kernel, 1.0 / math.sqrt(count * OWN * SITES)),
        out_shape=(
            jax.ShapeDtypeStruct((4, 4, OWN, SITES), f32),
            jax.ShapeDtypeStruct((HID, PACK), f32),
        ),
        in_specs=[pl.BlockSpec(memory_space=pltpu.SMEM)] + [vmem] * 9,
        out_specs=(vmem,) * 2,
        scratch_shapes=[
            pltpu.VMEM((GROUP, SITES), f32),
            pltpu.VMEM((4, ROWS, SITES), f32),
            pltpu.VMEM((4, OWN, SITES), f32),
            pltpu.VMEM((BANK, SITES), bf16),
            pltpu.VMEM((BANK, SITES), bf16),
            pltpu.VMEM((ROWS * HID, BANK), bf16),
            pltpu.VMEM((ROWS * HID, BANK), bf16),
            pltpu.VMEM((BANK, SITES), f32),
        ],
        compiler_params=pltpu.CompilerParams(vmem_limit_bytes=40 * 2**20),
    )(direction, gauge_links, halo, cotangent, mask, weight, table, head, cb, hb)

    depth = -(-HID // count)
    packed = jnp.pad(packed, ((0, count * depth - HID), (0, 0)))
    shape = (count, depth, PACK)
    summed = pl.pallas_call(
        partial(sum_kernel, count),
        out_shape=jax.ShapeDtypeStruct(shape, f32),
        in_specs=[vmem],
        out_specs=vmem,
        scratch_shapes=[pltpu.VMEM(shape, f32)] * 2
        + [pltpu.VMEM((depth, PACK), f32)]
        + [pltpu.SemaphoreType.DMA((count,))] * 4,
        compiler_params=pltpu.CompilerParams(collective_id=0, has_side_effects=True),
    )(packed.reshape(shape))
    summed = summed.reshape(count * depth, PACK)[:HID]
    return (
        grad,
        summed[:, :AT_CB],
        summed[:, AT_CB],
        summed[:, AT_HEAD:AT_HB].T,
        summed[:COEF, AT_HB],
    )


def solution(mesh):
    return jax.shard_map(
        body,
        mesh=mesh,
        in_specs=(
            P(None, None, ("groups", "ta"), None),
            P(None, None, ("groups", "ta"), None),
            P(),
            P(),
            P(),
            P(),
            P(("groups", "ta"), None),
            P(),
        ),
        out_specs=(
            P(None, None, ("groups", "ta"), None),
            P("groups", None),
            P("groups"),
            P("groups", None),
            P("groups"),
        ),
        check_vma=False,
    )
```

```python
from functools import partial
import math

import jax
import jax.numpy as jnp
import numpy as np
from jax import lax
from jax.experimental import pallas as pl
from jax.experimental.pallas import tpu as pltpu
from jax.sharding import PartitionSpec as P

LS = 8
SITES = LS**3
OWN = 8
REACH = 3
ROWS = 16
HID = 16
FEAT = 3
COEF = 10
SPACE_TAPS = 27
GROUP = FEAT * ROWS
BANK = 1408
AT_CB = 3 * SPACE_TAPS * FEAT
AT_HEAD = AT_CB + 1
AT_HB = AT_HEAD + COEF
PACK = 256
HIGH = lax.Precision.HIGHEST
NT = (((1,), (1,)), ((), ()))
TN = (((0,), (0,)), ((), ()))
NN = (((1,), (0,)), ((), ()))


def lane_roll(values, by):
    by = by % 128
    return jnp.concatenate(
        [pltpu.roll(values[:, at : at + 128], by, 1) for at in range(0, values.shape[1], 128)],
        axis=1,
    )


def moved(values, axis, offset):
    if axis == 0:
        return pltpu.roll(values, -offset % values.shape[0], 0)
    if axis == 1:
        return pltpu.roll(values, -offset * LS * LS % SITES, 1)
    stride = LS if axis == 2 else 1
    lane = lax.broadcasted_iota(jnp.int32, values.shape, 1)
    coordinate = (lane // stride) % LS
    wraps = coordinate == (LS - 1 if offset > 0 else 0)
    return jnp.where(
        wraps,
        lane_roll(values, offset * (LS - 1) * stride),
        lane_roll(values, -offset * stride),
    )


@partial(jax.custom_vjp, nondiff_argnums=(1, 2))
def shift(values, axis, offset):
    return moved(values, axis, offset)


shift.defvjp(
    lambda values, axis, offset: (moved(values, axis, offset), None),
    lambda axis, offset, _, grad: (moved(grad, axis, -offset),),
)


def q_shift(q, axis, offset):
    return tuple(shift(part, axis, offset) for part in q)


def q_mul(p, q):
    return (
        p[0] * q[0] - p[1] * q[1] - p[2] * q[2] - p[3] * q[3],
        p[0] * q[1] + p[1] * q[0] + p[2] * q[3] - p[3] * q[2],
        p[0] * q[2] - p[1] * q[3] + p[2] * q[0] + p[3] * q[1],
        p[0] * q[3] + p[1] * q[2] - p[2] * q[1] + p[3] * q[0],
    )


def q_conj(q):
    return (q[0], -q[1], -q[2], -q[3])


def staples(links, m):
    total = None
    for n in range(4):
        if n == m:
            continue
        ahead = q_shift(links[n], m, 1)
        upper = q_mul(q_mul(ahead, q_conj(q_shift(links[m], n, 1))), q_conj(links[n]))
        lower = q_shift(q_mul(q_conj(q_mul(links[m], ahead)), links[n]), n, -1)
        both = tuple(a + b for a, b in zip(upper, lower))
        total = both if total is None else tuple(a + b for a, b in zip(total, both))
    return total


def traces(links, m):
    others = [n for n in range(4) if n != m]
    out = []
    for i, j in ((0, 1), (0, 2), (1, 2)):
        a, b = others[i], others[j]
        left = q_mul(links[a], q_shift(links[b], a, 1))
        right = q_mul(links[b], q_shift(links[a], b, 1))
        out.append(sum(x * y for x, y in zip(left, right)))
    return tuple(out)


def cardinal(spot):
    rising = 0.5 * spot * spot
    middle = 0.5 * (-2.0 * spot * spot + 6.0 * spot - 3.0)
    falling = 0.5 * (3.0 - spot) * (3.0 - spot)
    return jnp.where(
        spot < 0.0,
        0.0,
        jnp.where(
            spot < 1.0, rising, jnp.where(spot < 2.0, middle, jnp.where(spot < 3.0, falling, 0.0))
        ),
    )


def rotate(link, staple, coeffs):
    loop = q_mul(link, staple)
    scaled = (loop[0] / 6.0 + 1.0) * (0.5 * (COEF - 2))
    strength = jnp.tanh(sum(coeffs[j] * cardinal(scaled - j + 2.0) for j in range(COEF)))
    turned = q_mul((jnp.zeros_like(loop[0]), loop[1], loop[2], loop[3]), link)
    length_sq = loop[1] * loop[1] + loop[2] * loop[2] + loop[3] * loop[3]
    scale = lax.rsqrt(1.0 + strength * strength * length_sq)
    return tuple((u + strength * v) * scale for u, v in zip(link, turned))


def halves(values):
    high = values.astype(jnp.bfloat16)
    return high, (values - high.astype(jnp.float32)).astype(jnp.bfloat16)


def dot3(a, b, dims):
    def one(x, y):
        return lax.dot_general(x, y, dims, preferred_element_type=jnp.float32)

    return one(a[0], b[0]) + (one(a[0], b[1]) + one(a[1], b[0]))


def group_roll(values, by):
    by = by % ROWS
    if by == 0:
        return values
    lane = lax.broadcasted_iota(jnp.int32, values.shape, 1) % ROWS
    return jnp.where(lane >= by, lane_roll(values, by), lane_roll(values, by - ROWS))


def kernel(
    scale, m_ref, links_ref, halo_ref, cot_ref, mask_ref, cw_ref, table_ref, head_ref, cb_ref,
    hb_ref, grad_ref, pack_ref,
    feat_ref, staple_ref, link_ref, bank_hi, bank_lo, big_hi, big_lo, dbank_ref,
):
    m = m_ref[0]

    def load(d):
        return tuple(
            jnp.concatenate([links_ref[d, c], halo_ref[4 * d + c]], axis=0) for c in range(4)
        )

    def slots(case):
        others = [n for n in range(4) if n != case]
        found = []
        for missing in reversed(others):
            k = jnp.where(m_ref[3] == missing, 0, jnp.where(m_ref[2] == missing, 1, 2))
            found.append(pl.ds(pl.multiple_of(k * ROWS, ROWS), ROWS))
        return found

    for case in range(4):

        @pl.when(m == case)
        def _(case=case):
            links = tuple(load(d) for d in range(4))
            for at, value in zip(slots(case), traces(links, case)):
                feat_ref[at, :] = value
            for c, value in enumerate(staples(links, case)):
                staple_ref[c] = value

    w0 = lax.dot_general(
        cw_ref[...], table_ref[...], NN, precision=HIGH, preferred_element_type=jnp.float32
    )
    for r in range(ROWS):
        high, low = halves(group_roll(w0, r))
        big_hi[r * HID : (r + 1) * HID, :] = high
        big_lo[r * HID : (r + 1) * HID, :] = low

    used = SPACE_TAPS * GROUP
    bank_hi[used:, :] = jnp.zeros((BANK - used, SITES), jnp.bfloat16)
    bank_lo[used:, :] = jnp.zeros((BANK - used, SITES), jnp.bfloat16)
    features = feat_ref[...]
    for c in (-1, 0, 1):
        third = moved(features, 3, c) if c else features
        for b in (-1, 0, 1):
            second = moved(third, 2, b) if b else third
            for a in (-1, 0, 1):
                first = moved(second, 1, a) if a else second
                e = ((a + 1) * 3 + b + 1) * 3 + c + 1
                high, low = halves(first)
                bank_hi[e * GROUP : (e + 1) * GROUP, :] = high
                bank_lo[e * GROUP : (e + 1) * GROUP, :] = low

    bank = (bank_hi[...], bank_lo[...])
    big = (big_hi[...], big_lo[...])
    hidden = jnp.tanh(dot3(big, bank, NN) + cb_ref[...])
    hidden2 = halves(hidden)
    head2 = halves(head_ref[...])
    coeffs = dot3(head2, hidden2, NN) + hb_ref[...]

    row = lax.broadcasted_iota(jnp.int32, (ROWS, SITES), 0)
    mask = jnp.concatenate([mask_ref[...].astype(jnp.float32), halo_ref[20]], axis=0)
    inside = (row <= OWN) | (row >= ROWS - 2)
    chosen = (mask != 0.0) & inside
    active = tuple(
        jnp.concatenate([links_ref[m, c], halo_ref[4 * m + c]], axis=0) for c in range(4)
    )
    cot = tuple(jnp.concatenate([cot_ref[m, c], halo_ref[16 + c]], axis=0) for c in range(4))
    _, pull = jax.vjp(
        rotate,
        active,
        tuple(staple_ref[c] for c in range(4)),
        tuple(coeffs[j * ROWS : (j + 1) * ROWS, :] for j in range(COEF)),
    )
    dlink, dstaple, dcoeff = pull(tuple(jnp.where(chosen, g, 0.0) for g in cot))
    for c in range(4):
        link_ref[c] = jnp.where(chosen, dlink[c], cot[c])[:OWN, :]
        staple_ref[c] = dstaple[c]
    dcoeff = jnp.concatenate(dcoeff, axis=0)
    dcoeff2 = halves(dcoeff)
    wide = lax.broadcasted_iota(jnp.int32, (ROWS * HID, COEF * ROWS), 1)
    tall = lax.broadcasted_iota(jnp.int32, (ROWS * HID, COEF * ROWS), 0)
    keep = (wide % ROWS == tall // HID) & (tall < OWN * HID)
    dhead = jnp.where(keep, dot3(hidden2, dcoeff2, NT), 0.0)
    dhead = sum(dhead[r * HID : (r + 1) * HID] for r in range(OWN))
    fold = (
        lax.broadcasted_iota(jnp.int32, (COEF * ROWS, 128), 0) // ROWS + (AT_HEAD - 128)
        == lax.broadcasted_iota(jnp.int32, (COEF * ROWS, 128), 1)
    ).astype(jnp.float32)
    extra = lax.dot_general(dhead, fold, NN, precision=HIGH, preferred_element_type=jnp.float32)
    own_sum = jnp.concatenate(
        [
            jnp.sum(dcoeff[j * ROWS : j * ROWS + OWN], axis=0, keepdims=True)
            for j in range(COEF)
        ]
        + [jnp.zeros((HID - COEF, SITES), jnp.float32)],
        axis=0,
    )
    column = lax.broadcasted_iota(jnp.int32, (HID, 128), 1)
    extra += jnp.where(column == AT_HB - 128, jnp.sum(own_sum, axis=1, keepdims=True), 0.0)

    dpre = dot3(head2, dcoeff2, TN) * (1.0 - hidden * hidden)
    own_pre = dpre[: OWN * HID]
    pre_sum = sum(own_pre[r * HID : (r + 1) * HID] for r in range(OWN))
    extra += jnp.where(column == AT_CB - 128, jnp.sum(pre_sum, axis=1, keepdims=True), 0.0)
    dpre2 = halves(dpre)
    dbig = dot3((dpre2[0][: OWN * HID], dpre2[1][: OWN * HID]), bank, NT)
    dw0 = sum(group_roll(dbig[r * HID : (r + 1) * HID], -r) for r in range(OWN))
    dw = lax.dot_general(
        dw0, table_ref[...], NT, precision=HIGH, preferred_element_type=jnp.float32
    )
    pack_ref[:, :128] = dw[:, :128] * scale
    pack_ref[:, 128:] = (dw[:, 128:] + extra) * scale

    dbank_ref[...] = dot3(big, dpre2, TN)
    dfeat = None
    for c in (-1, 0, 1):
        third = None
        for b in (-1, 0, 1):
            second = None
            for a in (-1, 0, 1):
                e = ((a + 1) * 3 + b + 1) * 3 + c + 1
                part = dbank_ref[e * GROUP : (e + 1) * GROUP, :]
                part = moved(part, 1, -a) if a else part
                second = part if second is None else second + part
            second = moved(second, 2, -b) if b else second
            third = second if third is None else third + second
        third = moved(third, 3, -c) if c else third
        dfeat = third if dfeat is None else dfeat + third
    feat_ref[...] = dfeat

    for case in range(4):

        @pl.when(m == case)
        def _(case=case):
            links = tuple(load(d) for d in range(4))
            _, back = jax.vjp(lambda u: (traces(u, case), staples(u, case)), links)
            (dlinks,) = back(
                (
                    tuple(feat_ref[at, :] for at in slots(case)),
                    tuple(staple_ref[c] for c in range(4)),
                )
            )
            for d in range(4):
                for c in range(4):
                    base = link_ref[c] if d == case else cot_ref[d, c]
                    grad_ref[d, c] = base + dlinks[d][c][:OWN, :]


def spread():
    table = np.zeros((PACK, BANK), np.float32)
    for a in range(3):
        for e in range(SPACE_TAPS):
            for k in range(FEAT):
                table[(a * SPACE_TAPS + e) * FEAT + k, e * GROUP + k * ROWS + (a - 1) % ROWS] = 1.0
    return table


def halo_kernel(
    n, m_ref, links_ref, cot_ref, mask_ref, halo_ref,
    head_ref, tail_ref, ahead_ref, behind_ref, send1, recv1, send2, recv2,
):
    me = lax.axis_index("ta")
    after, before = lax.rem(me + 1, n), lax.rem(me + n - 1, n)
    mesh_id = pl.DeviceIdType.MESH
    barrier = pltpu.get_barrier_semaphore()
    for neighbour in (before, after):
        pl.semaphore_signal(barrier, inc=1, device_id={"ta": neighbour}, device_id_type=mesh_id)
    m = m_ref[0]
    for msg_ref, start in ((head_ref, 0), (tail_ref, OWN - REACH)):
        rows = slice(start, start + REACH)
        for c in range(4):
            for d in range(4):
                msg_ref[4 * d + c] = links_ref[d, c][rows]
            msg_ref[16 + c] = cot_ref[m, c][rows]
        msg_ref[20] = mask_ref[...].astype(jnp.float32)[rows]
    pl.semaphore_wait(barrier, 2)
    down = pltpu.make_async_remote_copy(
        src_ref=head_ref, dst_ref=ahead_ref, send_sem=send1, recv_sem=recv1,
        device_id={"ta": before}, device_id_type=mesh_id,
    )
    up = pltpu.make_async_remote_copy(
        src_ref=tail_ref, dst_ref=behind_ref, send_sem=send2, recv_sem=recv2,
        device_id={"ta": after}, device_id_type=mesh_id,
    )
    down.start()
    up.start()
    down.wait()
    up.wait()
    gap = jnp.zeros((ROWS - OWN - 2 * REACH, SITES), jnp.float32)
    for c in range(21):
        halo_ref[c] = jnp.concatenate([ahead_ref[c], gap, behind_ref[c]], axis=0)


def sum_kernel(
    n, x_ref, out_ref, parts_ref, sums_ref, mine_ref, send1, recv1, send2, recv2
):
    me = lax.axis_index("ta")
    mesh_id = pl.DeviceIdType.MESH

    def to(k):
        return lax.rem(me + k, n)

    def scatter(k):
        return pltpu.make_async_remote_copy(
            src_ref=x_ref.at[to(k)],
            dst_ref=parts_ref.at[k],
            send_sem=send1.at[k],
            recv_sem=recv1.at[k],
            device_id={"ta": to(k)},
            device_id_type=mesh_id,
        )

    def gather(k):
        return pltpu.make_async_remote_copy(
            src_ref=mine_ref,
            dst_ref=sums_ref.at[k],
            send_sem=send2.at[k],
            recv_sem=recv2.at[k],
            device_id={"ta": to(k)},
            device_id_type=mesh_id,
        )

    def each(act):
        lax.fori_loop(1, n, lambda k, carry: (act(k), carry)[1], 0)

    barrier = pltpu.get_barrier_semaphore()
    each(
        lambda k: pl.semaphore_signal(
            barrier, inc=1, device_id={"ta": to(k)}, device_id_type=mesh_id
        )
    )
    pl.semaphore_wait(barrier, n - 1)
    each(lambda k: scatter(k).start())
    each(lambda k: scatter(k).wait_recv())
    total = x_ref[me]
    for k in range(1, n):
        total = total + parts_ref[k]
    mine_ref[...] = total
    each(lambda k: gather(k).start())
    out_ref[me] = total

    def keep(k):
        gather(k).wait_recv()
        out_ref[lax.rem(me + n - k, n)] = sums_ref[k]

    each(keep)
    each(lambda k: scatter(k).wait_send())
    each(lambda k: gather(k).wait_send())


def body(
    gauge_links, cotangent, conv_weight, conv_bias, head_weight, head_bias, site_mask, direction
):
    count = lax.axis_size("ta")
    vmem = pl.BlockSpec(memory_space=pltpu.VMEM)
    smem = pl.BlockSpec(memory_space=pltpu.SMEM)
    f32, bf16 = jnp.float32, jnp.bfloat16
    halo = pl.pallas_call(
        partial(halo_kernel, count),
        out_shape=jax.ShapeDtypeStruct((21, ROWS - OWN, SITES), f32),
        in_specs=[smem, vmem, vmem, vmem],
        out_specs=vmem,
        scratch_shapes=[pltpu.VMEM((21, REACH, SITES), f32)] * 4
        + [pltpu.SemaphoreType.DMA(())] * 4,
        compiler_params=pltpu.CompilerParams(collective_id=1, has_side_effects=True),
    )(direction, gauge_links, cotangent, site_mask)

    table = jnp.asarray(spread())
    weight = jnp.pad(conv_weight, ((0, 0), (0, PACK - AT_CB)))
    eye = jnp.eye(ROWS, dtype=jnp.float32)
    head = (head_weight[:, None, None, :] * eye[None, :, :, None]).reshape(
        COEF * ROWS, ROWS * HID
    )
    cb = jnp.tile(conv_bias, ROWS).reshape(ROWS * HID, 1)
    hb = jnp.repeat(head_bias, ROWS).reshape(COEF * ROWS, 1)

    grad, packed = pl.pallas_call(
        partial(kernel, 1.0 / math.sqrt(count * OWN * SITES)),
        out_shape=(
            jax.ShapeDtypeStruct((4, 4, OWN, SITES), f32),
            jax.ShapeDtypeStruct((HID, PACK), f32),
        ),
        in_specs=[smem] + [vmem] * 9,
        out_specs=(vmem,) * 2,
        scratch_shapes=[
            pltpu.VMEM((GROUP, SITES), f32),
            pltpu.VMEM((4, ROWS, SITES), f32),
            pltpu.VMEM((4, OWN, SITES), f32),
            pltpu.VMEM((BANK, SITES), bf16),
            pltpu.VMEM((BANK, SITES), bf16),
            pltpu.VMEM((ROWS * HID, BANK), bf16),
            pltpu.VMEM((ROWS * HID, BANK), bf16),
            pltpu.VMEM((BANK, SITES), f32),
        ],
        compiler_params=pltpu.CompilerParams(vmem_limit_bytes=40 * 2**20),
    )(direction, gauge_links, halo, cotangent, site_mask, weight, table, head, cb, hb)

    depth = -(-HID // count)
    packed = jnp.pad(packed, ((0, count * depth - HID), (0, 0)))
    shape = (count, depth, PACK)
    summed = pl.pallas_call(
        partial(sum_kernel, count),
        out_shape=jax.ShapeDtypeStruct(shape, f32),
        in_specs=[vmem],
        out_specs=vmem,
        scratch_shapes=[pltpu.VMEM(shape, f32)] * 2
        + [pltpu.VMEM((depth, PACK), f32)]
        + [pltpu.SemaphoreType.DMA((count,))] * 4,
        compiler_params=pltpu.CompilerParams(collective_id=0, has_side_effects=True),
    )(packed.reshape(shape))
    summed = summed.reshape(count * depth, PACK)[:HID]
    return (
        grad,
        summed[:, :AT_CB],
        summed[:, AT_CB],
        summed[:, AT_HEAD:AT_HB].T,
        summed[:COEF, AT_HB],
    )


def solution(mesh):
    return jax.shard_map(
        body,
        mesh=mesh,
        in_specs=(
            P(None, None, ("groups", "ta"), None),
            P(None, None, ("groups", "ta"), None),
            P(),
            P(),
            P(),
            P(),
            P(("groups", "ta"), None),
            P(),
        ),
        out_specs=(
            P(None, None, ("groups", "ta"), None),
            P("groups", None),
            P("groups"),
            P("groups", None),
            P("groups"),
        ),
        check_vma=False,
    )
```
